32 devices in a mesh: row: 4 (over x, core), col: 8 (over z, y).
Axes of the slice: x: 2, y: 2, z: 4, core: 2. Of those that a mesh axis runs over, the one named last changes fastest.
Arguments:
- rhs: float32 [24, 32768], P(None, 'col'), may hold values from -6 to 6
- noise_var: float32 [32768], P('col'), may hold values from 0.9 to 3.6
- block_rows: int32 [4, 4], P('row'), may hold values from 0 to 15, as said below
- kernel_blocks: bfloat16 [4, 8, 4, 2, 2048, 2048], P('row', 'col'), may hold values from -0.0078125 to 0.0078125
Outputs:
- solution_field: float32 [24, 32768], P(None, 'col')
- residual: float32 [24, 32768], P(None, 'col')
The draws below stay inside these ranges and needn't reach their ends.
Inputs may be any that keep to these rules, and one draw needn't show every extreme that they name: Each of the 16 block rows appears exactly once in block_rows.
All inputs are finite; a program needn't handle non-finite values.
Results may differ from the reference program's by a relative error of at most 0.024.
Values may be sent and summed in bfloat16 or wider, within the bound.
A program may use at most 192 MiB of HBM per device.

```python
import math
import jax
import jax.numpy as jnp
from jax import lax

BLK = 2048
NBLK = 16
RHS = 24
ITERS = 8
ORDER = 32768
RB = 4
CB = 2
N_ROW = 4
N_COL = 8


def draw_block_rows(key, part):
    order = jax.random.permutation(jax.random.fold_in(key, 11), NBLK)
    return order.astype(jnp.int32).reshape(-1, RB)


def draw_kernel_blocks(key, part):
    shape = (N_ROW, N_COL, RB, CB, BLK, BLK)
    scale = 1.0 / math.sqrt(8.0 * NBLK * BLK)
    values = jnp.clip(jax.random.normal(jax.random.fold_in(key, 5), shape, jnp.float32), -4.0, 4.0)
    return (values * scale).astype(jnp.bfloat16)


def block_levels(own_key, shape, shards, least, high):
    gain, own = 1.0, jax.random.fold_in(own_key, 6)
    for axis_at, parts in shards:
        heights = jnp.exp(jax.random.uniform(jax.random.fold_in(own, axis_at), (parts,), jnp.float32, least / len(shards), high / len(shards)))
        gain = gain * jnp.repeat(heights, shape[axis_at] // parts).reshape([-1 if axis == axis_at else 1 for axis in range(len(shape))])
    return gain


def gaussian(rng, dims, deviation, bound, shards=(), held_as=jnp.bfloat16):
    factor_of = block_levels(rng, dims, shards, -0.22, 0.18) if shards else 1.0
    array = jax.random.normal(rng, dims, jnp.float32) * deviation * factor_of
    return jnp.minimum(jnp.maximum(array, -bound), bound).astype(held_as)


def setup_inputs(seed: int = 0) -> dict:
    splits = jax.random.split(jax.random.key(seed), 5)
    return {
        "rhs": gaussian(splits[0], (RHS, ORDER), 1.0, 6.0, ((1, 8),), jnp.float32),
        "noise_var": jnp.clip(jnp.exp(math.log(3.6) - 1.3862944 * jax.random.uniform(splits[1], (ORDER,), jnp.float32) ** block_levels(splits[1], (ORDER,), ((0, 8),), -0.2, 0.2)), 0.9, 3.6),
        "block_rows": draw_block_rows(jax.random.fold_in(splits[4], 71), 0),
        "kernel_blocks": draw_kernel_blocks(jax.random.fold_in(splits[4], 71), 0),
    }


def reference(rhs, noise_var, block_rows, kernel_blocks):
    slot_total = N_ROW * N_COL * RB * CB
    row_ids = jnp.broadcast_to(block_rows[:, None, :, None], (N_ROW, N_COL, RB, CB)).reshape(slot_total).astype(jnp.int32)
    col_grid = jnp.arange(N_COL, dtype=jnp.int32)[:, None, None] * CB + jnp.arange(CB, dtype=jnp.int32)[None, None, :]
    col_ids = jnp.broadcast_to(col_grid[None], (N_ROW, N_COL, RB, CB)).reshape(slot_total).astype(jnp.int32)
    flat_blocks = kernel_blocks.reshape(slot_total, BLK, BLK)

    def operate(direction):
        dir_bf = direction.astype(jnp.bfloat16)

        def slot_step(image, item):
            block, row_id, col_id = item
            weight = (col_id >= row_id).astype(jnp.float32)
            row_start = (row_id * BLK).astype(jnp.int32)
            col_start = (col_id * BLK).astype(jnp.int32)
            col_piece = lax.dynamic_slice_in_dim(dir_bf, col_start, BLK, 1)
            row_piece = lax.dynamic_slice_in_dim(dir_bf, row_start, BLK, 1)
            forward = jnp.dot(col_piece, block.T, preferred_element_type=jnp.float32) * weight
            mirrored = jnp.dot(row_piece, block, preferred_element_type=jnp.float32) * weight
            current = lax.dynamic_slice_in_dim(image, row_start, BLK, 1)
            image = lax.dynamic_update_slice_in_dim(image, current + forward, row_start, 1)
            current = lax.dynamic_slice_in_dim(image, col_start, BLK, 1)
            image = lax.dynamic_update_slice_in_dim(image, current + mirrored, col_start, 1)
            return image, None

        image, _ = lax.scan(slot_step, noise_var[None, :] * direction, (flat_blocks, row_ids, col_ids))
        return image

    solution_field = jnp.zeros_like(rhs)
    residual = rhs
    direction = rhs
    norm_now = jnp.sum(residual * residual, axis=1)
    for step in range(ITERS):
        image = operate(direction)
        curvature = jnp.sum(direction * image, axis=1)
        alpha = norm_now / curvature
        solution_field = solution_field + alpha[:, None] * direction
        residual = residual - alpha[:, None] * image
        norm_next = jnp.sum(residual * residual, axis=1)
        direction = residual + (norm_next / norm_now)[:, None] * direction
        norm_now = norm_next
    return solution_field, residual
```

```python
import functools

import jax
import jax.numpy as jnp
from jax import lax
from jax.experimental import pallas as pl
from jax.experimental.pallas import tpu as pltpu
from jax.sharding import PartitionSpec as P

ITERS = 8
RESIDENT = 6
ROWS = 512
STEP = 256
MESH = pl.DeviceIdType.MESH
F32 = jnp.float32
BF16 = jnp.bfloat16


def cg_kernel(
    n_row, n_col, rb, cb, width, resident,
    rows_ref, rhs_ref, noise_ref, k_hbm,
    x_ref, r_ref,
    kres, kbuf, d, dall, vj, vi, facc, fbf, frecv, rsum, macc, th, hrecv, xrecv, im, srecv,
    ksem, bsem, ds, dr, gs, gr, fs, fr, as_, ar, hs, hr, xs, xr, cs, cr, ss, sr,
):
    slots = rb * cb
    slab = cb * width
    half = slab // 2
    chunk = rb * width // n_col
    n_x = n_row // 2
    vectors = rhs_ref.shape[0]
    per = width // ROWS
    streamed = (slots - resident) * per
    held = resident * per
    row = lax.axis_index("row")
    col = lax.axis_index("col")
    core = lax.rem(row, 2)
    xg = row // 2
    mate = row + 1 - 2 * core

    def column(j):
        return lax.rem(col + j, n_col)

    def source(j):
        return lax.rem(col - j + n_col, n_col)

    def x_row(j):
        return lax.rem(xg + j, n_x) * 2 + core

    def x_from(j):
        return lax.rem(xg - j + n_x, n_x)

    def remote(src, dst, send, recv, to):
        return pltpu.make_async_remote_copy(
            src_ref=src, dst_ref=dst, send_sem=send, recv_sem=recv, device_id=to, device_id_type=MESH
        )

    def each(lo, hi, body):
        def step(j, carry):
            body(j)
            return carry

        lax.fori_loop(lo, hi, step, 0)

    def d_send(j):
        at = dall.at[2 * col + core]
        return remote(at, at, ds.at[j], dr.at[j], (row, column(j)))

    def d_recv(j):
        at = dall.at[2 * source(j) + core]
        return remote(at, at, ds.at[j], dr.at[j], (row, column(j)))

    def g_send(j):
        at = dall.at[2 * source(j) + core]
        return remote(at, at, gs.at[j], gr.at[j], (mate, col))

    def g_recv(j):
        at = dall.at[2 * source(j) + 1 - core]
        return remote(at, at, gs.at[j], gr.at[j], (mate, col))

    def f_copy(j):
        return remote(fbf.at[column(j)], frecv.at[j], fs.at[j], fr.at[j], (row, column(j)))

    def a_send(j):
        return remote(rsum.at[col], rsum.at[col], as_.at[j], ar.at[j], (row, column(j)))

    def a_recv(j):
        at = rsum.at[source(j)]
        return remote(at, at, as_.at[j], ar.at[j], (row, column(j)))

    def s_send(j):
        return remote(srecv.at[col], srecv.at[col], ss.at[j], sr.at[j], (row, column(j)))

    def s_recv(j):
        at = srecv.at[source(j)]
        return remote(at, at, ss.at[j], sr.at[j], (row, column(j)))

    def slot_load(s):
        return pltpu.make_async_copy(k_hbm.at[s], kres.at[s], ksem.at[s])

    def stream(i):
        s = resident + i // per
        at = pl.multiple_of(lax.rem(i, per) * ROWS, ROWS)
        b = lax.rem(i, 2)
        return pltpu.make_async_copy(k_hbm.at[s, pl.ds(at, ROWS), :], kbuf.at[b], bsem.at[b])

    barrier = pltpu.get_barrier_semaphore()
    each(1, n_col, lambda j: pl.semaphore_signal(barrier, inc=1, device_id=(row, column(j)), device_id_type=MESH))
    pl.semaphore_signal(barrier, inc=1, device_id=(mate, col), device_id_type=MESH)
    for j in range(1, n_x):
        pl.semaphore_signal(barrier, inc=1, device_id=(x_row(j), col), device_id_type=MESH)

    each(0, resident, lambda s: slot_load(s).start())
    x_ref[...] = jnp.zeros_like(x_ref)
    r_ref[...] = rhs_ref[...]
    d[...] = rhs_ref[...]
    for h in range(2):
        dall[2 * col + h] = d[:, h * half : (h + 1) * half].astype(BF16)
    pl.semaphore_wait(barrier, n_col + n_x - 1)

    def forward(block, s, at):
        k = s // cb
        facc[k, :, pl.ds(at, ROWS)] += lax.dot_general(
            vj[s], block, (((1,), (1,)), ((), ())), preferred_element_type=F32
        )

    def mirror(block, s, at):
        m = lax.rem(s, cb)
        macc[m] += jnp.dot(vi[s, :, pl.ds(at, ROWS)], block, preferred_element_type=F32)

    def over(product, lo, hi, first=None):
        def resident_piece(u):
            s = u // per
            at = pl.multiple_of(lax.rem(u, per) * ROWS, ROWS)
            if first is not None:

                @pl.when(jnp.logical_and(first, lax.rem(u, per) == 0))
                def _():
                    slot_load(s).wait()

            product(kres[s, pl.ds(at, ROWS), :], s, at)

        if streamed == 0:
            each(lo, hi, resident_piece)
            return
        share = held // streamed

        def step(i):
            for q in range(share):
                resident_piece(i * share + q)
            stream(i).wait()
            product(kbuf[lax.rem(i, 2)], resident + i // per, pl.multiple_of(lax.rem(i, per) * ROWS, ROWS))

            @pl.when(i + 2 < streamed)
            def _():
                stream(i + 2).start()

        each(lo, hi, step)

    steps = streamed if streamed else held

    def prefetch():
        if streamed:
            stream(0).start()
            stream(1).start()

    def iteration(t, carry):
        each(1, n_col, lambda j: d_send(j).start())
        facc[...] = jnp.zeros_like(facc)
        macc[...] = jnp.zeros_like(macc)
        prefetch()
        for s in range(slots):
            k, m = s // cb, s % cb
            used = (col * cb + m >= rows_ref[0, k]).astype(F32)
            vj[s] = (d[:, m * width : (m + 1) * width] * used).astype(BF16)
        over(forward, 0, steps, t == 0)
        for c in range(n_col):
            k, at = c * chunk // width, c * chunk % width
            fbf[c] = facc[k, :, at : at + chunk].astype(BF16)
        each(1, n_col, lambda j: f_copy(j).start())
        prefetch()

        def pass_on(j):
            d_recv(j).wait_recv()
            g_send(j).start()

        each(1, n_col, pass_on)
        each(1, n_col, lambda j: g_recv(j).wait_recv())
        pieces = width // half if half < width else 1
        for s in range(slots):
            k, m = s // cb, s % cb
            used = (col * cb + m >= rows_ref[0, k]).astype(F32)
            span = width // pieces
            for p in range(pieces):
                part = dall[rows_ref[0, k] * pieces + p].astype(F32) * used
                vi[s, :, p * span : (p + 1) * span] = part.astype(BF16)
        over(mirror, 0, steps // 2)
        total = fbf[col].astype(F32)
        for j in range(1, n_col):
            f_copy(j).wait_recv()
            total = total + frecv[j].astype(F32)
        rsum[col] = total.astype(BF16)
        each(1, n_col, lambda j: a_send(j).start())
        over(mirror, steps // 2, steps)
        each(1, n_col, lambda j: a_recv(j).wait_recv())

        for h in range(2):
            m, off = h * half // width, h * half % width
            block = col * cb + m
            piece = min(chunk, half)
            for q in range(half // piece):
                at = off + q * piece
                value = macc[m, :, at : at + piece]
                for k in range(rb):
                    c, inner = (k * width + at) // chunk, (k * width + at) % chunk
                    select = (rows_ref[0, k] == block).astype(F32)
                    value = value + rsum[c, :, inner : inner + piece].astype(F32) * select
                th[h, :, q * piece : (q + 1) * piece] = value

        give = remote(th.at[1 - core], hrecv, hs, hr, (mate, col))
        give.start()
        give.wait()
        par = lax.rem(t, 2)
        xrecv[par, xg] = th[core] + hrecv[...]
        for j in range(1, n_x):
            at = xrecv.at[par, xg]
            remote(at, at, xs.at[j], xr.at[par, j], (x_row(j), col)).start()
        for j in range(1, n_x):
            at = xrecv.at[par, x_from(j)]
            remote(at, at, xs.at[j], xr.at[par, j], (x_row(j), col)).wait()
        value = xrecv[par, 0]
        for q in range(1, n_x):
            value = value + xrecv[par, q]
        im[core] = value
        mine, other = im.at[core], im.at[1 - core]
        remote(mine, mine, cs, cr, (mate, col)).start()
        back = remote(other, other, cs, cr, (mate, col))
        back.wait()

        sums = [jnp.zeros((vectors, STEP), F32) for _ in range(4)]
        for q in range(slab // STEP):
            at = q * STEP
            h, inner = at // half, at % half
            dd, rr = d[:, at : at + STEP], r_ref[:, at : at + STEP]
            ii = noise_ref[:, at : at + STEP] * dd + im[h, :, inner : inner + STEP]
            im[h, :, inner : inner + STEP] = ii
            sums = [sums[0] + dd * ii, sums[1] + rr * ii, sums[2] + ii * ii, sums[3] + rr * rr]
        lane = lax.broadcasted_iota(jnp.int32, (vectors, 128), 1)
        pay = jnp.zeros((vectors, 128), F32)
        for q in range(4):
            pay = jnp.where(lane == q, jnp.sum(sums[q], axis=1, keepdims=True), pay)
        srecv[col] = pay
        each(1, n_col, lambda j: g_send(j).wait_send())
        each(1, n_col, lambda j: s_send(j).start())
        each(1, n_col, lambda j: s_recv(j).wait_recv())

        def sent(j):
            d_send(j).wait_send()
            f_copy(j).wait_send()
            a_send(j).wait_send()
            s_send(j).wait_send()

        each(1, n_col, sent)
        total = srecv[0]
        for q in range(1, n_col):
            total = total + srecv[q]
        curvature, cross, square, norm = [total[:, q : q + 1] for q in range(4)]
        alpha = norm / curvature
        after = norm - 2.0 * alpha * cross + alpha * alpha * square
        beta = after / norm
        for q in range(slab // STEP):
            at = q * STEP
            h, inner = at // half, at % half
            dd = d[:, at : at + STEP]
            x_ref[:, at : at + STEP] += alpha * dd
            rr = r_ref[:, at : at + STEP] - alpha * im[h, :, inner : inner + STEP]
            r_ref[:, at : at + STEP] = rr
            dd = rr + beta * dd
            d[:, at : at + STEP] = dd
            dall[2 * col + h, :, inner : inner + STEP] = dd.astype(BF16)
        return carry

    lax.fori_loop(0, ITERS, iteration, 0)


def on_device(n_row, n_col, rhs, noise_var, block_rows, kernel_blocks):
    rb, cb, width = kernel_blocks.shape[2], kernel_blocks.shape[3], kernel_blocks.shape[4]
    vectors, slab = rhs.shape
    slots, half, chunk, n_x = rb * cb, slab // 2, rb * width // n_col, n_row // 2
    resident = min(RESIDENT, slots)
    dma = pltpu.SemaphoreType.DMA
    vmem = pl.BlockSpec(memory_space=pltpu.VMEM)
    return pl.pallas_call(
        functools.partial(cg_kernel, n_row, n_col, rb, cb, width, resident),
        out_shape=[jax.ShapeDtypeStruct((vectors, slab), F32)] * 2,
        in_specs=[pl.BlockSpec(memory_space=pltpu.SMEM), vmem, vmem, pl.BlockSpec(memory_space=pl.ANY)],
        out_specs=[vmem, vmem],
        scratch_shapes=[
            pltpu.VMEM((resident, width, width), BF16),
            pltpu.VMEM((2, ROWS, width), BF16),
            pltpu.VMEM((vectors, slab), F32),
            pltpu.VMEM((2 * n_col, vectors, half), BF16),
            pltpu.VMEM((slots, vectors, width), BF16),
            pltpu.VMEM((slots, vectors, width), BF16),
            pltpu.VMEM((rb, vectors, width), F32),
            pltpu.VMEM((n_col, vectors, chunk), BF16),
            pltpu.VMEM((n_col, vectors, chunk), BF16),
            pltpu.VMEM((n_col, vectors, chunk), BF16),
            pltpu.VMEM((cb, vectors, width), F32),
            pltpu.VMEM((2, vectors, half), F32),
            pltpu.VMEM((vectors, half), F32),
            pltpu.VMEM((2, n_x, vectors, half), F32),
            pltpu.VMEM((2, vectors, half), F32),
            pltpu.VMEM((n_col, vectors, 128), F32),
            dma((resident,)), dma((2,)),
            dma((n_col,)), dma((n_col,)),
            dma((n_col,)), dma((n_col,)),
            dma((n_col,)), dma((n_col,)),
            dma((n_col,)), dma((n_col,)),
            dma, dma,
            dma((n_x,)), dma((2, n_x)),
            dma, dma,
            dma((n_col,)), dma((n_col,)),
        ],
        compiler_params=pltpu.CompilerParams(
            collective_id=0, has_side_effects=True, vmem_limit_bytes=63 * 1024 * 1024
        ),
        cost_estimate=pl.CostEstimate(
            flops=ITERS * slots * 4 * vectors * width * width,
            bytes_accessed=slots * width * width * 2,
            transcendentals=0,
        ),
    )(block_rows, rhs, noise_var.reshape(1, slab), kernel_blocks.reshape(slots, width, width))


def solution(mesh):
    return jax.shard_map(
        functools.partial(on_device, mesh.shape["row"], mesh.shape["col"]),
        mesh=mesh,
        in_specs=(P(None, "col"), P("col"), P("row", None), P("row", "col", None, None, None, None)),
        out_specs=(P(None, "col"), P(None, "col")),
        check_vma=False,
    )
```

```python
import functools

import jax
import jax.numpy as jnp
from jax import lax
from jax.experimental import pallas as pl
from jax.experimental.pallas import tpu as pltpu
from jax.sharding import PartitionSpec as P

ITERS = 8
RESIDENT = 6
ROWS = 512
STEP = 256
MESH = pl.DeviceIdType.MESH
F32 = jnp.float32
BF16 = jnp.bfloat16


def cg_kernel(
    n_row, n_col, rb, cb, width, resident,
    rows_ref, rhs_ref, noise_ref, k_hbm,
    x_ref, r_ref,
    kres, kbuf, d, dall, vj, vi, facc, fbf, frecv, rsum, macc, th, hrecv, xrecv, im, srecv,
    ksem, bsem, ds, dr, gs, gr, fs, fr, as_, ar, hs, hr, xs, xr, cs, cr, ss, sr,
):
    slots = rb * cb
    slab = cb * width
    half = slab // 2
    chunk = rb * width // n_col
    n_x = n_row // 2
    vectors = rhs_ref.shape[0]
    per = width // ROWS
    streamed = (slots - resident) * per
    held = resident * per
    row = lax.axis_index("row")
    col = lax.axis_index("col")
    core = lax.rem(row, 2)
    xg = row // 2
    mate = row + 1 - 2 * core

    def column(j):
        return lax.rem(col + j, n_col)

    def source(j):
        return lax.rem(col - j + n_col, n_col)

    def x_row(j):
        return lax.rem(xg + j, n_x) * 2 + core

    def x_from(j):
        return lax.rem(xg - j + n_x, n_x)

    def remote(src, dst, send, recv, to):
        return pltpu.make_async_remote_copy(
            src_ref=src, dst_ref=dst, send_sem=send, recv_sem=recv, device_id=to, device_id_type=MESH
        )

    def each(lo, hi, body):
        def step(j, carry):
            body(j)
            return carry

        lax.fori_loop(lo, hi, step, 0)

    def d_send(j):
        at = dall.at[2 * col + core]
        return remote(at, at, ds.at[j], dr.at[j], (row, column(j)))

    def d_recv(j):
        at = dall.at[2 * source(j) + core]
        return remote(at, at, ds.at[j], dr.at[j], (row, column(j)))

    def g_send(j):
        at = dall.at[2 * source(j) + core]
        return remote(at, at, gs.at[j], gr.at[j], (mate, col))

    def g_recv(j):
        at = dall.at[2 * source(j) + 1 - core]
        return remote(at, at, gs.at[j], gr.at[j], (mate, col))

    def f_copy(j):
        return remote(fbf.at[column(j)], frecv.at[j], fs.at[j], fr.at[j], (row, column(j)))

    def a_send(j):
        return remote(rsum.at[col], rsum.at[col], as_.at[j], ar.at[j], (row, column(j)))

    def a_recv(j):
        at = rsum.at[source(j)]
        return remote(at, at, as_.at[j], ar.at[j], (row, column(j)))

    def s_send(j):
        return remote(srecv.at[col], srecv.at[col], ss.at[j], sr.at[j], (row, column(j)))

    def s_recv(j):
        at = srecv.at[source(j)]
        return remote(at, at, ss.at[j], sr.at[j], (row, column(j)))

    def slot_load(s):
        return pltpu.make_async_copy(k_hbm.at[s], kres.at[s], ksem.at[s])

    def stream(i):
        s = resident + i // per
        at = pl.multiple_of(lax.rem(i, per) * ROWS, ROWS)
        b = lax.rem(i, 2)
        return pltpu.make_async_copy(k_hbm.at[s, pl.ds(at, ROWS), :], kbuf.at[b], bsem.at[b])

    barrier = pltpu.get_barrier_semaphore()
    each(1, n_col, lambda j: pl.semaphore_signal(barrier, inc=1, device_id=(row, column(j)), device_id_type=MESH))
    pl.semaphore_signal(barrier, inc=1, device_id=(mate, col), device_id_type=MESH)
    for j in range(1, n_x):
        pl.semaphore_signal(barrier, inc=1, device_id=(x_row(j), col), device_id_type=MESH)

    each(0, resident, lambda s: slot_load(s).start())
    x_ref[...] = jnp.zeros_like(x_ref)
    r_ref[...] = rhs_ref[...]
    d[...] = rhs_ref[...]
    for h in range(2):
        dall[2 * col + h] = d[:, h * half : (h + 1) * half].astype(BF16)
    pl.semaphore_wait(barrier, n_col + n_x - 1)

    def forward(block, s, at):
        k = s // cb
        facc[k, :, pl.ds(at, ROWS)] += lax.dot_general(
            vj[s], block, (((1,), (1,)), ((), ())), preferred_element_type=F32
        )

    def mirror(block, s, at):
        m = lax.rem(s, cb)
        macc[m] += jnp.dot(vi[s, :, pl.ds(at, ROWS)], block, preferred_element_type=F32)

    def over(product, lo, hi, first=None, beside=None):
        def resident_piece(u):
            s = u // per
            at = pl.multiple_of(lax.rem(u, per) * ROWS, ROWS)
            if first is not None:

                @pl.when(jnp.logical_and(first, lax.rem(u, per) == 0))
                def _():
                    slot_load(s).wait()

            product(kres[s, pl.ds(at, ROWS), :], s, at)

        if streamed == 0:

            def only(i):
                resident_piece(i)
                if beside is not None:
                    beside(i)

            each(lo, hi, only)
            return
        share = held // streamed

        def step(i):
            for q in range(share):
                resident_piece(i * share + q)
            stream(i).wait()
            product(kbuf[lax.rem(i, 2)], resident + i // per, pl.multiple_of(lax.rem(i, per) * ROWS, ROWS))

            @pl.when(i + 2 < streamed)
            def _():
                stream(i + 2).start()

            if beside is not None:
                beside(i)

        each(lo, hi, step)

    steps = streamed if streamed else held

    def prefetch():
        if streamed:
            stream(0).start()
            stream(1).start()

    def iteration(t, carry):
        each(1, n_col, lambda j: d_send(j).start())
        facc[...] = jnp.zeros_like(facc)
        macc[...] = jnp.zeros_like(macc)
        prefetch()
        for s in range(slots):
            k, m = s // cb, s % cb
            used = (col * cb + m >= rows_ref[0, k]).astype(F32)
            vj[s] = (d[:, m * width : (m + 1) * width] * used).astype(BF16)

        def pass_on(j):
            d_recv(j).wait_recv()
            g_send(j).start()

        def share_out(i):
            each(1 + (n_col - 1) * i // steps, 1 + (n_col - 1) * (i + 1) // steps, pass_on)

        over(forward, 0, steps, t == 0, share_out)
        for c in range(n_col):
            k, at = c * chunk // width, c * chunk % width
            fbf[c] = facc[k, :, at : at + chunk].astype(BF16)
        each(1, n_col, lambda j: f_copy(j).start())
        prefetch()

        each(1, n_col, lambda j: g_recv(j).wait_recv())
        pieces = width // half if half < width else 1
        for s in range(slots):
            k, m = s // cb, s % cb
            used = (col * cb + m >= rows_ref[0, k]).astype(F32)
            span = width // pieces
            for p in range(pieces):
                part = dall[rows_ref[0, k] * pieces + p].astype(F32) * used
                vi[s, :, p * span : (p + 1) * span] = part.astype(BF16)
        over(mirror, 0, steps // 2)
        total = fbf[col].astype(F32)
        for j in range(1, n_col):
            f_copy(j).wait_recv()
            total = total + frecv[j].astype(F32)
        rsum[col] = total.astype(BF16)
        each(1, n_col, lambda j: a_send(j).start())
        over(mirror, steps // 2, steps)
        each(1, n_col, lambda j: a_recv(j).wait_recv())

        for h in range(2):
            m, off = h * half // width, h * half % width
            block = col * cb + m
            piece = min(chunk, half)
            for q in range(half // piece):
                at = off + q * piece
                value = macc[m, :, at : at + piece]
                for k in range(rb):
                    c, inner = (k * width + at) // chunk, (k * width + at) % chunk
                    select = (rows_ref[0, k] == block).astype(F32)
                    value = value + rsum[c, :, inner : inner + piece].astype(F32) * select
                th[h, :, q * piece : (q + 1) * piece] = value

        give = remote(th.at[1 - core], hrecv, hs, hr, (mate, col))
        give.start()
        give.wait()
        par = lax.rem(t, 2)
        xrecv[par, xg] = (th[core] + hrecv[...]).astype(BF16)
        for j in range(1, n_x):
            at = xrecv.at[par, xg]
            remote(at, at, xs.at[j], xr.at[par, j], (x_row(j), col)).start()
        for j in range(1, n_x):
            at = xrecv.at[par, x_from(j)]
            remote(at, at, xs.at[j], xr.at[par, j], (x_row(j), col)).wait()
        value = xrecv[par, 0].astype(F32)
        for q in range(1, n_x):
            value = value + xrecv[par, q].astype(F32)
        im[core] = value
        mine, other = im.at[core], im.at[1 - core]
        remote(mine, mine, cs, cr, (mate, col)).start()
        back = remote(other, other, cs, cr, (mate, col))
        back.wait()

        sums = [jnp.zeros((vectors, STEP), F32) for _ in range(4)]
        for q in range(slab // STEP):
            at = q * STEP
            h, inner = at // half, at % half
            dd, rr = d[:, at : at + STEP], r_ref[:, at : at + STEP]
            ii = noise_ref[:, at : at + STEP] * dd + im[h, :, inner : inner + STEP]
            im[h, :, inner : inner + STEP] = ii
            sums = [sums[0] + dd * ii, sums[1] + rr * ii, sums[2] + ii * ii, sums[3] + rr * rr]
        lane = lax.broadcasted_iota(jnp.int32, (vectors, 128), 1)
        pay = jnp.zeros((vectors, 128), F32)
        for q in range(4):
            pay = jnp.where(lane == q, jnp.sum(sums[q], axis=1, keepdims=True), pay)
        srecv[col] = pay
        each(1, n_col, lambda j: g_send(j).wait_send())
        each(1, n_col, lambda j: s_send(j).start())
        each(1, n_col, lambda j: s_recv(j).wait_recv())

        def sent(j):
            d_send(j).wait_send()
            f_copy(j).wait_send()
            a_send(j).wait_send()
            s_send(j).wait_send()

        each(1, n_col, sent)
        total = srecv[0]
        for q in range(1, n_col):
            total = total + srecv[q]
        curvature, cross, square, norm = [total[:, q : q + 1] for q in range(4)]
        alpha = norm / curvature
        after = norm - 2.0 * alpha * cross + alpha * alpha * square
        beta = after / norm
        for q in range(slab // STEP):
            at = q * STEP
            h, inner = at // half, at % half
            dd = d[:, at : at + STEP]
            x_ref[:, at : at + STEP] += alpha * dd
            rr = r_ref[:, at : at + STEP] - alpha * im[h, :, inner : inner + STEP]
            r_ref[:, at : at + STEP] = rr
            dd = rr + beta * dd
            d[:, at : at + STEP] = dd
            dall[2 * col + h, :, inner : inner + STEP] = dd.astype(BF16)
        return carry

    lax.fori_loop(0, ITERS, iteration, 0)


def on_device(n_row, n_col, rhs, noise_var, block_rows, kernel_blocks):
    rb, cb, width = kernel_blocks.shape[2], kernel_blocks.shape[3], kernel_blocks.shape[4]
    vectors, slab = rhs.shape
    slots, half, chunk, n_x = rb * cb, slab // 2, rb * width // n_col, n_row // 2
    resident = min(RESIDENT, slots)
    dma = pltpu.SemaphoreType.DMA
    vmem = pl.BlockSpec(memory_space=pltpu.VMEM)
    return pl.pallas_call(
        functools.partial(cg_kernel, n_row, n_col, rb, cb, width, resident),
        out_shape=[jax.ShapeDtypeStruct((vectors, slab), F32)] * 2,
        in_specs=[pl.BlockSpec(memory_space=pltpu.SMEM), vmem, vmem, pl.BlockSpec(memory_space=pl.ANY)],
        out_specs=[vmem, vmem],
        scratch_shapes=[
            pltpu.VMEM((resident, width, width), BF16),
            pltpu.VMEM((2, ROWS, width), BF16),
            pltpu.VMEM((vectors, slab), F32),
            pltpu.VMEM((2 * n_col, vectors, half), BF16),
            pltpu.VMEM((slots, vectors, width), BF16),
            pltpu.VMEM((slots, vectors, width), BF16),
            pltpu.VMEM((rb, vectors, width), F32),
            pltpu.VMEM((n_col, vectors, chunk), BF16),
            pltpu.VMEM((n_col, vectors, chunk), BF16),
            pltpu.VMEM((n_col, vectors, chunk), BF16),
            pltpu.VMEM((cb, vectors, width), F32),
            pltpu.VMEM((2, vectors, half), F32),
            pltpu.VMEM((vectors, half), F32),
            pltpu.VMEM((2, n_x, vectors, half), BF16),
            pltpu.VMEM((2, vectors, half), F32),
            pltpu.VMEM((n_col, vectors, 128), F32),
            dma((resident,)), dma((2,)),
            dma((n_col,)), dma((n_col,)),
            dma((n_col,)), dma((n_col,)),
            dma((n_col,)), dma((n_col,)),
            dma((n_col,)), dma((n_col,)),
            dma, dma,
            dma((n_x,)), dma((2, n_x)),
            dma, dma,
            dma((n_col,)), dma((n_col,)),
        ],
        compiler_params=pltpu.CompilerParams(
            collective_id=0, has_side_effects=True, vmem_limit_bytes=63 * 1024 * 1024
        ),
        cost_estimate=pl.CostEstimate(
            flops=ITERS * slots * 4 * vectors * width * width,
            bytes_accessed=slots * width * width * 2,
            transcendentals=0,
        ),
    )(block_rows, rhs, noise_var.reshape(1, slab), kernel_blocks.reshape(slots, width, width))


def solution(mesh):
    return jax.shard_map(
        functools.partial(on_device, mesh.shape["row"], mesh.shape["col"]),
        mesh=mesh,
        in_specs=(P(None, "col"), P("col"), P("row", None), P("row", "col", None, None, None, None)),
        out_specs=(P(None, "col"), P(None, "col")),
        check_vma=False,
    )
```
